32 devices in a mesh: dp: 2 (over x), ctx: 4 (over z), tp: 4 (over y, core).
Axes of the slice: x: 2, y: 2, z: 4, core: 2. Of those that a mesh axis runs over, the one named last changes fastest.
Arguments:
- queries: bfloat16 [1024, 4096], P(('dp', 'ctx'), 'tp'), parts along dimension 0, may hold values from -25 to 25
- keys: bfloat16 [1024, 1024], P(('dp', 'ctx'), 'tp'), parts along dimension 0, may hold values from -6 to 6
- values: bfloat16 [1024, 1024], P(('dp', 'ctx'), 'tp'), parts along dimension 0, may hold values from -6 to 6
- counts: int32 [8, 4], P('dp'), parts along dimension 0, may hold values from 0 to 64, as said below
- doc_lengths: int32 [32], P('dp'), parts along dimension 0, may hold values from 1 to 256, 512 in all
Outputs:
- attended: bfloat16 [1024, 4096], P(('dp', 'ctx'), 'tp'), parts along dimension 0
The draws below stay inside these ranges and needn't reach their ends.
There are 2 independent parts, one for each index of `dp`. The reference program is written for one: setup_inputs(seed, part) draws one part's arguments, and reference() takes and returns one part's arrays. A program takes and returns all parts, laid end to end along the dimension named above; each array names one. Nothing has to cross between parts.
Inputs may be any that keep to these rules, and one draw needn't show every extreme that they name: Every row and every column of counts sums to 128; no entry exceeds 64, and some entry equals 64.
All inputs are finite; a program needn't handle non-finite values.
Results may differ from the reference program's by a relative error of at most 0.006.
Values may be sent and summed in bfloat16 or wider, within the bound.
A program may use at most 64 MiB of HBM per device.

```python
import math
import jax
import jax.numpy as jnp
import numpy as np
from jax import lax

HQ = 32
KVH = 8
HD = 128
TOK_DEV = 128
DOCS = 16
SEQ = 512
HALF = 64
N_CTX = 4


def draw_queries(key, part):
    base = jnp.clip(jax.random.normal(jax.random.fold_in(key, 1), (SEQ, HQ, HD), jnp.float32), -6.0, 6.0)
    return base.reshape(SEQ, HQ * HD).astype(jnp.bfloat16)


def draw_keys(key, part):
    base = jnp.clip(jax.random.normal(jax.random.fold_in(key, 2), (SEQ, KVH, HD), jnp.float32), -6.0, 6.0)
    return base.reshape(SEQ, KVH * HD).astype(jnp.bfloat16)


def draw_counts(key, part):
    mean_rows = TOK_DEV // N_CTX
    wobble = jax.random.randint(jax.random.fold_in(key, 21), (N_CTX,), 0, mean_rows + 1)
    wobble = wobble.at[0].set(mean_rows).at[N_CTX - 1].set(0)
    profile = mean_rows + wobble - jnp.roll(wobble, 1)
    owner_perm = jax.random.permutation(jax.random.fold_in(key, 22), N_CTX)
    loader_perm = jax.random.permutation(jax.random.fold_in(key, 23), N_CTX)
    shift = (owner_perm[None, :] - loader_perm[:, None]) % N_CTX
    return jnp.take(profile, shift).astype(jnp.int32)


def shard_levels(rng, extent, shards, low, top_value):
    factor_of, own = 1.0, jax.random.fold_in(rng, 6)
    for position, blocks in shards:
        draws = jnp.exp(jax.random.uniform(jax.random.fold_in(own, position), (blocks,), jnp.float32, low / len(shards), top_value / len(shards)))
        factor_of = factor_of * jnp.repeat(draws, extent[position] // blocks).reshape([-1 if axis == position else 1 for axis in range(len(extent))])
    return factor_of


def split_up(number_of, total, bound, skew):
    loads = [(1 << 20) // math.isqrt(standing ** skew) + 1 for standing in range(2, number_of + 1)]
    surplus, holding = total - bound - (number_of - 1), [1] * (number_of - 1)
    while surplus > 0:
        candidates = [i for i in range(number_of - 1) if holding[i] < bound]
        pool, left = sum([loads[i] for i in candidates]), surplus
        for i in candidates:
            extra = min(bound - holding[i], max(1, left * loads[i] // pool), surplus)
            holding[i] = holding[i] + extra
            surplus = surplus - extra
    return np.array([bound] + holding)


def ragged_sizes(key, count, total, bound, lean):
    if count == 2:
        one = jax.random.randint(key, (), max(1, total - bound), min(bound, total - 1) + 1)
        return jnp.stack([one, total - one])
    sizes = jnp.asarray(split_up(count, total, bound, lean), jnp.int32)
    couples = (count - 1) // 2
    donor, receiver = sizes[1:1 + 2 * couples:2], sizes[2:2 + 2 * couples:2]
    room = jnp.minimum(donor - 1, bound - receiver)
    shifted = jax.random.randint(jax.random.fold_in(key, 1), (couples,), 0, 1 << 20) % (room + 1)
    sizes = sizes.at[1:1 + 2 * couples:2].set(donor - shifted).at[2:2 + 2 * couples:2].set(receiver + shifted)
    return sizes[jax.random.permutation(jax.random.fold_in(key, 2), count)]


def scatter_about(stream_key, extent, scale, reach, split=(), held_as=jnp.bfloat16):
    array = scale * jax.random.normal(stream_key, extent, jnp.float32)
    if split:
        array = array * shard_levels(stream_key, extent, split, -0.22, 0.18)
    return jnp.clip(array, -reach, reach).astype(held_as)


def setup_inputs(seed: int = 0, part: int = 0) -> dict:
    arg_keys = jax.random.split(jax.random.key(seed), 6)
    own_keys = jax.random.split(jax.random.fold_in(arg_keys[5], part), 6)
    return {
        "queries": draw_queries(jax.random.fold_in(jax.random.fold_in(arg_keys[5], part), 71), part),
        "keys": draw_keys(jax.random.fold_in(jax.random.fold_in(arg_keys[5], part), 71), part),
        "values": scatter_about(own_keys[2], (SEQ, KVH * HD), 1.0, 6.0, ((0, 4), (1, 4))),
        "counts": draw_counts(jax.random.fold_in(jax.random.fold_in(arg_keys[5], part), 71), part),
        "doc_lengths": ragged_sizes(own_keys[4], DOCS, SEQ, SEQ // 2, 2).astype(jnp.int32),
    }


def span_pos(owner, local):
    return jnp.where(local < HALF, owner * HALF + local, (2 * N_CTX - 1 - owner) * HALF + local - HALF).astype(jnp.int32)


def loader_positions(counts):
    counts = counts.astype(jnp.int32)
    ends = jnp.cumsum(counts, axis=1).astype(jnp.int32)
    starts = ends - counts
    before = (jnp.cumsum(counts, axis=0) - counts).astype(jnp.int32)
    rowids = jnp.arange(TOK_DEV, dtype=jnp.int32)
    owner = jnp.sum((ends[:, None, :] <= rowids[None, :, None]).astype(jnp.int32), axis=2).astype(jnp.int32)
    start_sel = jnp.take_along_axis(starts, owner, axis=1)
    pre_sel = jnp.take_along_axis(before, owner, axis=1)
    return span_pos(owner, pre_sel + rowids[None, :] - start_sel)


def reference(queries, keys, values, counts, doc_lengths):
    group = HQ // KVH
    where_to = loader_positions(counts).reshape(-1)
    packed_q = jnp.zeros((SEQ, HQ * HD), jnp.bfloat16).at[where_to].set(queries)
    packed_k = jnp.zeros((SEQ, KVH * HD), jnp.bfloat16).at[where_to].set(keys)
    packed_v = jnp.zeros((SEQ, KVH * HD), jnp.bfloat16).at[where_to].set(values)
    doc_ends = jnp.cumsum(doc_lengths.astype(jnp.int32)).astype(jnp.int32)
    places = jnp.arange(SEQ, dtype=jnp.int32)
    segment = jnp.sum((doc_ends[None, :] <= places[:, None]).astype(jnp.int32), axis=1).astype(jnp.int32)
    key_full = packed_k.reshape(SEQ, KVH, HD).astype(jnp.float32)
    value_full = packed_v.reshape(SEQ, KVH, HD).astype(jnp.float32)
    scale = 1.0 / (HD ** 0.5)
    block = 128

    def one_block(index):
        first = (index * block).astype(jnp.int32)
        query_rows = lax.dynamic_slice_in_dim(packed_q, first, block, 0)
        query_rows = query_rows.reshape(block, KVH, group, HD).astype(jnp.float32)
        qpos = first + jnp.arange(block, dtype=jnp.int32)
        qseg = lax.dynamic_slice_in_dim(segment, first, block, 0)
        visible = (places[None, :] <= qpos[:, None]) & (segment[None, :] == qseg[:, None])
        scores = jnp.einsum("qcgd,kcd->cgqk", query_rows, key_full) * scale
        masked = jnp.where(visible, scores, -1e30)
        top = jnp.max(masked, axis=-1, keepdims=True)
        expo = jnp.where(visible, jnp.exp(masked - top), 0.0)
        total = jnp.sum(expo, axis=-1)
        weights = expo.astype(jnp.bfloat16).astype(jnp.float32)
        mixed = jnp.einsum("cgqk,kcd->cgqd", weights, value_full) / total[..., None]
        return jnp.transpose(mixed, (2, 0, 1, 3)).reshape(block, HQ * HD).astype(jnp.bfloat16)

    packed_out = lax.map(one_block, jnp.arange(SEQ // block, dtype=jnp.int32)).reshape(SEQ, HQ * HD)
    owners = jnp.arange(N_CTX, dtype=jnp.int32)[:, None]
    locals_ = jnp.arange(TOK_DEV, dtype=jnp.int32)[None, :]
    own_index = span_pos(owners + 0 * locals_, locals_ + 0 * owners).reshape(-1)
    return jnp.take(packed_out, own_index, axis=0)
```

```python
import functools
import math

import jax
import jax.numpy as jnp
from jax import lax
from jax.experimental import pallas as pl
from jax.experimental.pallas import tpu as pltpu
from jax.sharding import PartitionSpec as P

HQ = 32
KVH = 8
HD = 128
MESH = pl.DeviceIdType.MESH


def span_pos(owner, local, half, n):
    return jnp.where(
        local < half, owner * half + local, (2 * n - 1 - owner) * half + local - half
    )


def kernel(
    n,
    counts,
    docs,
    q_ref,
    k_ref,
    v_ref,
    out_ref,
    qsend,
    qbuf,
    kbuf,
    vbuf,
    bias,
    pick,
    qown,
    q_send_sem,
    q_recv_sem,
    kv_send_sem,
    kv_recv_sem,
):
    me = lax.axis_index("ctx")
    tok = q_ref.shape[0]
    half = tok // 2
    slot = qsend.shape[1]
    kv_local = k_ref.shape[1] // HD
    group = HQ // KVH

    barrier = pltpu.get_barrier_semaphore()
    for d in range(1, n):
        pl.semaphore_signal(
            barrier, inc=1, device_id={"ctx": lax.rem(me + d, n)}, device_id_type=MESH
        )

    row_ids = lax.broadcasted_iota(jnp.int32, (slot, tok), 1)
    row_js = lax.broadcasted_iota(jnp.int32, (slot, tok), 0)
    start = jnp.int32(0)
    for o in range(n):
        onehot = (row_ids == row_js + start).astype(jnp.bfloat16)
        qsend[o] = jnp.dot(onehot, q_ref[...], preferred_element_type=jnp.float32).astype(
            jnp.bfloat16
        )
        start = start + counts[me, o]

    pl.semaphore_wait(barrier, n - 1)

    def kv_copies(direction, d):
        sign = 1 if direction == 0 else -1
        source = me - sign * d
        target = me + sign
        result = []
        for which, (own, held) in enumerate(((k_ref, kbuf), (v_ref, vbuf))):
            result.append(
                pltpu.make_async_remote_copy(
                    src_ref=own if d == 0 else held.at[source],
                    dst_ref=held.at[source],
                    send_sem=kv_send_sem.at[which, direction, d],
                    recv_sem=kv_recv_sem.at[which, source],
                    device_id={"ctx": target},
                    device_id_type=MESH,
                )
            )
        return result

    def sends(direction, d):
        if direction == 0:
            return (me - d >= 0) & (me < n - 1)
        return (me + d < n) & (me > 0)

    def receives(direction, d):
        return (me - d >= 0) if direction == 0 else (me + d < n)

    for direction in (0, 1):

        @pl.when(sends(direction, 0))
        def _():
            for copy in kv_copies(direction, 0):
                copy.start()

    q_copies = []
    for d in range(n - 1, 0, -1):
        target = lax.rem(me + d, n)
        copy = pltpu.make_async_remote_copy(
            src_ref=qsend.at[target],
            dst_ref=qbuf.at[me],
            send_sem=q_send_sem.at[d],
            recv_sem=q_recv_sem.at[me],
            device_id={"ctx": target},
            device_id_type=MESH,
        )
        copy.start()
        q_copies.append(copy)

    qbuf[me] = qsend[me]
    kbuf[me] = k_ref[...]
    vbuf[me] = v_ref[...]

    local = lax.broadcasted_iota(jnp.int32, (tok, tok), 0)
    lane = lax.broadcasted_iota(jnp.int32, (1, tok), 1)
    query_pos = span_pos(me, local, half, n)
    doc_start = jnp.zeros((tok, tok), jnp.int32)
    end = jnp.int32(0)
    for d in range(docs.shape[0]):
        end = end + docs[d]
        doc_start = jnp.where(query_pos >= end, end, doc_start)
    before = [jnp.int32(0)] * n
    take_q = lax.broadcasted_iota(jnp.int32, (tok, slot), 0)
    take_j = lax.broadcasted_iota(jnp.int32, (tok, slot), 1)
    mine_before = jnp.int32(0)
    for l in range(n):
        start = jnp.int32(0)
        key_pos = jnp.zeros((1, tok), jnp.int32)
        for o in range(n):
            pos = span_pos(jnp.int32(o), lane + (before[o] - start), half, n)
            key_pos = jnp.where(lane >= start, pos, key_pos)
            start = start + counts[l, o]
            before[o] = before[o] + counts[l, o]
        visible = (key_pos <= query_pos) & (key_pos >= doc_start)
        bias[:, l * tok : (l + 1) * tok] = jnp.where(visible, 0.0, -1e30)
        mine = counts[l, me]
        pick[l] = ((take_q == take_j + mine_before) & (take_j < mine)).astype(jnp.bfloat16)
        mine_before = mine_before + mine

    for d in range(1, n):
        for direction in (0, 1):

            @pl.when(receives(direction, d))
            def _():
                source = me - d if direction == 0 else me + d
                for which, (own, held) in enumerate(((k_ref, kbuf), (v_ref, vbuf))):
                    pltpu.make_async_remote_copy(
                        src_ref=own,
                        dst_ref=held.at[source],
                        send_sem=kv_send_sem.at[which, direction, 0],
                        recv_sem=kv_recv_sem.at[which, source],
                        device_id={"ctx": me},
                        device_id_type=MESH,
                    ).wait_recv()

            if d < n - 1:

                @pl.when(sends(direction, d))
                def _():
                    for copy in kv_copies(direction, d):
                        copy.start()

    for d in range(1, n):
        source = lax.rem(me + d, n)
        pltpu.make_async_remote_copy(
            src_ref=qsend.at[source],
            dst_ref=qbuf.at[source],
            send_sem=q_send_sem.at[0],
            recv_sem=q_recv_sem.at[source],
            device_id={"ctx": me},
            device_id_type=MESH,
        ).wait_recv()

    own = jnp.zeros((tok, q_ref.shape[1]), jnp.float32)
    for l in range(n):
        own = own + jnp.dot(pick[l], qbuf[l], preferred_element_type=jnp.float32)
    qown[...] = own.astype(jnp.bfloat16)

    factor = math.log2(math.e) / math.sqrt(HD)
    seq = n * tok
    width = min(seq, 512)
    per = width // tok
    for c in range(kv_local):
        for g in range(group):
            h = c * group + g
            query = qown[:, h * HD : (h + 1) * HD]
            top = total = acc = None
            for b in range(seq // width):
                key = kbuf[b * per : (b + 1) * per, :, c * HD : (c + 1) * HD].reshape(width, HD)
                value = vbuf[b * per : (b + 1) * per, :, c * HD : (c + 1) * HD].reshape(width, HD)
                score = lax.dot_general(
                    query, key, (((1,), (1,)), ((), ())), preferred_element_type=jnp.float32
                )
                score = score * factor + bias[:, b * width : (b + 1) * width]
                peak = jnp.max(score, axis=1, keepdims=True)
                new = peak if b == 0 else jnp.maximum(top, peak)
                expo = jnp.exp2(score - new)
                part = jnp.sum(expo, axis=1, keepdims=True)
                mixed = jnp.dot(
                    expo.astype(jnp.bfloat16), value, preferred_element_type=jnp.float32
                )
                if b == 0:
                    total, acc = part, mixed
                else:
                    keep = jnp.exp2(top - new)
                    total = total * keep + part
                    acc = acc * keep + mixed
                top = new
            out_ref[:, h * HD : (h + 1) * HD] = (acc / total).astype(jnp.bfloat16)

    for copy in q_copies:
        copy.wait_send()
    for d in range(n - 1):
        for direction in (0, 1):

            @pl.when(sends(direction, d))
            def _():
                for copy in kv_copies(direction, d):
                    copy.wait_send()


def body(queries, keys, values, counts, doc_lengths):
    n = lax.axis_size("ctx")
    tok, wide = queries.shape
    narrow = keys.shape[1]
    slot = max(16, 2 * tok // n)
    vmem = pl.BlockSpec(memory_space=pltpu.VMEM)
    smem = pl.BlockSpec(memory_space=pltpu.SMEM)
    return pl.pallas_call(
        functools.partial(kernel, n),
        out_shape=jax.ShapeDtypeStruct((tok, wide), jnp.bfloat16),
        in_specs=[smem, smem, vmem, vmem, vmem],
        out_specs=vmem,
        scratch_shapes=[
            pltpu.VMEM((n, slot, wide), jnp.bfloat16),
            pltpu.VMEM((n, slot, wide), jnp.bfloat16),
            pltpu.VMEM((n, tok, narrow), jnp.bfloat16),
            pltpu.VMEM((n, tok, narrow), jnp.bfloat16),
            pltpu.VMEM((tok, n * tok), jnp.float32),
            pltpu.VMEM((n, tok, slot), jnp.bfloat16),
            pltpu.VMEM((tok, wide), jnp.bfloat16),
            pltpu.SemaphoreType.DMA((n,)),
            pltpu.SemaphoreType.DMA((n,)),
            pltpu.SemaphoreType.DMA((2, 2, n)),
            pltpu.SemaphoreType.DMA((2, n)),
        ],
        compiler_params=pltpu.CompilerParams(
            collective_id=0, has_side_effects=True, vmem_limit_bytes=32 * 1024 * 1024
        ),
    )(counts, doc_lengths, queries, keys, values)


def solution(mesh):
    placed = (
        P(("dp", "ctx"), "tp"),
        P(("dp", "ctx"), "tp"),
        P(("dp", "ctx"), "tp"),
        P("dp", None),
        P("dp"),
    )
    return jax.shard_map(
        body, mesh=mesh, in_specs=placed, out_specs=P(("dp", "ctx"), "tp"), check_vma=False
    )
```

```python
import functools
import math

import jax
import jax.numpy as jnp
from jax import lax
from jax.experimental import pallas as pl
from jax.experimental.pallas import tpu as pltpu
from jax.sharding import PartitionSpec as P

HQ = 32
KVH = 8
HD = 128
MESH = pl.DeviceIdType.MESH


def span_pos(owner, local, half, n):
    return jnp.where(
        local < half, owner * half + local, (2 * n - 1 - owner) * half + local - half
    )


def kernel(
    n,
    counts_in,
    docs_in,
    q_in,
    k_in,
    v_in,
    out_ref,
    counts,
    docs,
    q_ref,
    qsend,
    qbuf,
    kbuf,
    vbuf,
    bias,
    pick,
    qown,
    q_send_sem,
    q_recv_sem,
    kv_send_sem,
    kv_recv_sem,
    load_sem,
):
    me = lax.axis_index("ctx")
    tok = q_ref.shape[0]
    half = tok // 2
    slot = qsend.shape[1]
    kv_local = kbuf.shape[2] // HD
    group = HQ // KVH

    barrier = pltpu.get_barrier_semaphore()
    for d in range(1, n):
        pl.semaphore_signal(
            barrier, inc=1, device_id={"ctx": lax.rem(me + d, n)}, device_id_type=MESH
        )

    loads = [
        pltpu.make_async_copy(source, target, load_sem.at[i])
        for i, (source, target) in enumerate(
            (
                (k_in, kbuf.at[me]),
                (v_in, vbuf.at[me]),
                (counts_in, counts),
                (docs_in, docs),
                (q_in, q_ref),
            )
        )
    ]
    for load in loads:
        load.start()

    def kv_copies(direction, d):
        sign = 1 if direction == 0 else -1
        source = me - sign * d
        target = me + sign
        return [
            pltpu.make_async_remote_copy(
                src_ref=held.at[source],
                dst_ref=held.at[source],
                send_sem=kv_send_sem.at[which, direction, d],
                recv_sem=kv_recv_sem.at[which, source],
                device_id={"ctx": target},
                device_id_type=MESH,
            )
            for which, held in enumerate((kbuf, vbuf))
        ]

    def sends(direction, d):
        if direction == 0:
            return (me - d >= 0) & (me < n - 1)
        return (me + d < n) & (me > 0)

    def receives(direction, d):
        return (me - d >= 0) if direction == 0 else (me + d < n)

    def pass_on(d):
        for direction in (0, 1):

            @pl.when(sends(direction, d))
            def _():
                for copy in kv_copies(direction, d):
                    copy.start()

    def q_copy(direction, d):
        target = me + d if direction == 0 else me - d
        return pltpu.make_async_remote_copy(
            src_ref=qsend.at[target],
            dst_ref=qbuf.at[me],
            send_sem=q_send_sem.at[direction, d],
            recv_sem=q_recv_sem.at[me],
            device_id={"ctx": target},
            device_id_type=MESH,
        )

    def send_q(d):
        for direction in (0, 1):

            @pl.when(receives(1 - direction, d))
            def _():
                q_copy(direction, d).start()

    pl.semaphore_wait(barrier, n - 1)
    loads[0].wait()
    loads[1].wait()
    pass_on(0)
    for load in loads[2:]:
        load.wait()

    row_ids = lax.broadcasted_iota(jnp.int32, (slot, tok), 1)
    row_js = lax.broadcasted_iota(jnp.int32, (slot, tok), 0)
    start = jnp.int32(0)
    for o in range(n):
        onehot = (row_ids == row_js + start).astype(jnp.bfloat16)
        qsend[o] = jnp.dot(onehot, q_ref[...], preferred_element_type=jnp.float32).astype(
            jnp.bfloat16
        )
        start = start + counts[me, o]

    for d in range(n - 1, 1, -1):
        send_q(d)

    qbuf[me] = qsend[me]

    local = lax.broadcasted_iota(jnp.int32, (tok, tok), 0)
    lane = lax.broadcasted_iota(jnp.int32, (1, tok), 1)
    query_pos = span_pos(me, local, half, n)
    doc_start = jnp.zeros((tok, tok), jnp.int32)
    end = jnp.int32(0)
    for d in range(docs.shape[0]):
        end = end + docs[d]
        doc_start = jnp.where(query_pos >= end, end, doc_start)
    before = [jnp.int32(0)] * n
    take_q = lax.broadcasted_iota(jnp.int32, (tok, slot), 0)
    take_j = lax.broadcasted_iota(jnp.int32, (tok, slot), 1)
    mine_before = jnp.int32(0)
    for l in range(n):
        start = jnp.int32(0)
        key_pos = jnp.zeros((1, tok), jnp.int32)
        for o in range(n):
            pos = span_pos(jnp.int32(o), lane + (before[o] - start), half, n)
            key_pos = jnp.where(lane >= start, pos, key_pos)
            start = start + counts[l, o]
            before[o] = before[o] + counts[l, o]
        visible = (key_pos <= query_pos) & (key_pos >= doc_start)
        bias[:, l * tok : (l + 1) * tok] = jnp.where(visible, 0.0, -1e30)
        mine = counts[l, me]
        pick[l] = ((take_q == take_j + mine_before) & (take_j < mine)).astype(jnp.bfloat16)
        mine_before = mine_before + mine

    for d in range(1, n):
        for direction in (0, 1):

            @pl.when(receives(direction, d))
            def _():
                source = me - d if direction == 0 else me + d
                for which, held in enumerate((kbuf, vbuf)):
                    pltpu.make_async_remote_copy(
                        src_ref=held.at[source],
                        dst_ref=held.at[source],
                        send_sem=kv_send_sem.at[which, direction, 0],
                        recv_sem=kv_recv_sem.at[which, source],
                        device_id={"ctx": me},
                        device_id_type=MESH,
                    ).wait_recv()

        if d < n - 1:
            pass_on(d)
        if d == 1:
            send_q(1)

    for d in range(1, n):
        source = lax.rem(me + d, n)
        pltpu.make_async_remote_copy(
            src_ref=qsend.at[source],
            dst_ref=qbuf.at[source],
            send_sem=q_send_sem.at[0, 0],
            recv_sem=q_recv_sem.at[source],
            device_id={"ctx": me},
            device_id_type=MESH,
        ).wait_recv()

    own = jnp.zeros((tok, q_ref.shape[1]), jnp.float32)
    for l in range(n):
        own = own + jnp.dot(pick[l], qbuf[l], preferred_element_type=jnp.float32)
    qown[...] = own.astype(jnp.bfloat16)

    factor = math.log2(math.e) / math.sqrt(HD)
    seq = n * tok
    width = min(seq, 512)
    per = width // tok
    for c in range(kv_local):
        for g in range(group):
            h = c * group + g
            query = qown[:, h * HD : (h + 1) * HD]
            top = total = acc = None
            for b in range(seq // width):
                key = kbuf[b * per : (b + 1) * per, :, c * HD : (c + 1) * HD].reshape(width, HD)
                value = vbuf[b * per : (b + 1) * per, :, c * HD : (c + 1) * HD].reshape(width, HD)
                score = lax.dot_general(
                    query, key, (((1,), (1,)), ((), ())), preferred_element_type=jnp.float32
                )
                score = score * factor + bias[:, b * width : (b + 1) * width]
                peak = jnp.max(score, axis=1, keepdims=True)
                new = peak if b == 0 else jnp.maximum(top, peak)
                expo = jnp.exp2(score - new)
                part = jnp.sum(expo, axis=1, keepdims=True)
                mixed = jnp.dot(
                    expo.astype(jnp.bfloat16), value, preferred_element_type=jnp.float32
                )
                if b == 0:
                    total, acc = part, mixed
                else:
                    keep = jnp.exp2(top - new)
                    total = total * keep + part
                    acc = acc * keep + mixed
                top = new
            out_ref[:, h * HD : (h + 1) * HD] = (acc / total).astype(jnp.bfloat16)

    for d in range(1, n):
        for direction in (0, 1):

            @pl.when(receives(1 - direction, d))
            def _():
                q_copy(direction, d).wait_send()

    for d in range(n - 1):
        for direction in (0, 1):

            @pl.when(sends(direction, d))
            def _():
                for copy in kv_copies(direction, d):
                    copy.wait_send()


def body(queries, keys, values, counts, doc_lengths):
    n = lax.axis_size("ctx")
    tok, wide = queries.shape
    narrow = keys.shape[1]
    slot = max(16, 2 * tok // n)
    vmem = pl.BlockSpec(memory_space=pltpu.VMEM)
    anywhere = pl.BlockSpec(memory_space=pl.ANY)
    return pl.pallas_call(
        functools.partial(kernel, n),
        out_shape=jax.ShapeDtypeStruct((tok, wide), jnp.bfloat16),
        in_specs=[anywhere] * 5,
        out_specs=vmem,
        scratch_shapes=[
            pltpu.SMEM(counts.shape, jnp.int32),
            pltpu.SMEM(doc_lengths.shape, jnp.int32),
            pltpu.VMEM((tok, wide), jnp.bfloat16),
            pltpu.VMEM((n, slot, wide), jnp.bfloat16),
            pltpu.VMEM((n, slot, wide), jnp.bfloat16),
            pltpu.VMEM((n, tok, narrow), jnp.bfloat16),
            pltpu.VMEM((n, tok, narrow), jnp.bfloat16),
            pltpu.VMEM((tok, n * tok), jnp.float32),
            pltpu.VMEM((n, tok, slot), jnp.bfloat16),
            pltpu.VMEM((tok, wide), jnp.bfloat16),
            pltpu.SemaphoreType.DMA((2, n)),
            pltpu.SemaphoreType.DMA((n,)),
            pltpu.SemaphoreType.DMA((2, 2, n)),
            pltpu.SemaphoreType.DMA((2, n)),
            pltpu.SemaphoreType.DMA((5,)),
        ],
        compiler_params=pltpu.CompilerParams(
            collective_id=0, has_side_effects=True, vmem_limit_bytes=56 * 1024 * 1024
        ),
    )(counts, doc_lengths, queries, keys, values)


def solution(mesh):
    placed = (
        P(("dp", "ctx"), "tp"),
        P(("dp", "ctx"), "tp"),
        P(("dp", "ctx"), "tp"),
        P("dp", None),
        P("dp"),
    )
    return jax.shard_map(
        body, mesh=mesh, in_specs=placed, out_specs=P(("dp", "ctx"), "tp"), check_vma=False
    )
```

```python
import functools
import math

import jax
import jax.numpy as jnp
from jax import lax
from jax.experimental import pallas as pl
from jax.experimental.pallas import tpu as pltpu
from jax.sharding import PartitionSpec as P

HQ = 32
KVH = 8
HD = 128
PART = 2 * HD
MESH = pl.DeviceIdType.MESH


def span_pos(owner, local, half, n):
    return jnp.where(
        local < half, owner * half + local, (2 * n - 1 - owner) * half + local - half
    )


def kernel(
    n,
    counts_in,
    docs_in,
    q_in,
    k_in,
    v_in,
    out_ref,
    counts,
    docs,
    q_ref,
    qsend,
    qbuf,
    kbuf,
    vbuf,
    bias,
    pick,
    q_send_sem,
    q_recv_sem,
    kv_send_sem,
    kv_recv_sem,
    load_sem,
):
    me = lax.axis_index("ctx")
    tok = q_ref.shape[0]
    half = tok // 2
    slot = qsend.shape[2]
    parts = q_ref.shape[1] // PART
    group = HQ // KVH

    barrier = pltpu.get_barrier_semaphore()
    for d in range(1, n):
        pl.semaphore_signal(
            barrier, inc=1, device_id={"ctx": lax.rem(me + d, n)}, device_id_type=MESH
        )

    loads = [
        pltpu.make_async_copy(source, target, load_sem.at[i])
        for i, (source, target) in enumerate(
            (
                (k_in, kbuf.at[me]),
                (v_in, vbuf.at[me]),
                (counts_in, counts),
                (docs_in, docs),
                (q_in, q_ref),
            )
        )
    ]
    for load in loads:
        load.start()

    def kv_copies(direction, d):
        sign = 1 if direction == 0 else -1
        source = me - sign * d
        target = me + sign
        return [
            pltpu.make_async_remote_copy(
                src_ref=held.at[source],
                dst_ref=held.at[source],
                send_sem=kv_send_sem.at[which, direction, d],
                recv_sem=kv_recv_sem.at[which, source],
                device_id={"ctx": target},
                device_id_type=MESH,
            )
            for which, held in enumerate((kbuf, vbuf))
        ]

    def sends(direction, d):
        if direction == 0:
            return (me - d >= 0) & (me < n - 1)
        return (me + d < n) & (me > 0)

    def receives(direction, d):
        return (me - d >= 0) if direction == 0 else (me + d < n)

    def wait_kv(direction, d):
        source = me - d if direction == 0 else me + d
        for which, held in enumerate((kbuf, vbuf)):
            pltpu.make_async_remote_copy(
                src_ref=held.at[source],
                dst_ref=held.at[source],
                send_sem=kv_send_sem.at[which, direction, 0],
                recv_sem=kv_recv_sem.at[which, source],
                device_id={"ctx": me},
                device_id_type=MESH,
            ).wait_recv()

    def pass_on(d):
        for direction in (0, 1):

            @pl.when(sends(direction, d))
            def _():
                if d > 0:
                    wait_kv(direction, d)
                for copy in kv_copies(direction, d):
                    copy.start()

    def q_copy(direction, d, p):
        target = me + d if direction == 0 else me - d
        return pltpu.make_async_remote_copy(
            src_ref=qsend.at[p, target],
            dst_ref=qbuf.at[p, me],
            send_sem=q_send_sem.at[p, direction, d],
            recv_sem=q_recv_sem.at[p, me],
            device_id={"ctx": target},
            device_id_type=MESH,
        )

    def send_q(p):
        for d in range(n - 1, 0, -1):
            for direction in (0, 1):

                @pl.when(receives(1 - direction, d))
                def _():
                    q_copy(direction, d, p).start()

    pl.semaphore_wait(barrier, n - 1)
    loads[0].wait()
    loads[1].wait()
    pass_on(0)
    for load in loads[2:]:
        load.wait()

    row_ids = lax.broadcasted_iota(jnp.int32, (slot, tok), 1)
    row_js = lax.broadcasted_iota(jnp.int32, (slot, tok), 0)
    start = jnp.int32(0)
    onehots = []
    for o in range(n):
        onehots.append((row_ids == row_js + start).astype(jnp.bfloat16))
        start = start + counts[me, o]
    onehot = jnp.concatenate(onehots, axis=0)

    def pack_q(p):
        packed = jnp.dot(
            onehot, q_ref[:, p * PART : (p + 1) * PART], preferred_element_type=jnp.float32
        )
        qsend[p] = packed.astype(jnp.bfloat16).reshape(n, slot, PART)
        qbuf[p, me] = qsend[p, me]

    for p in range(parts):
        pack_q(p)
        if p == 0:
            send_q(0)
    sent = 1
    for d in range(1, n - 1):
        pass_on(d)
        if sent < parts:
            send_q(sent)
            sent += 1
    for p in range(sent, parts):
        send_q(p)

    local = lax.broadcasted_iota(jnp.int32, (tok, tok), 0)
    lane = lax.broadcasted_iota(jnp.int32, (1, tok), 1)
    query_pos = span_pos(me, local, half, n)
    doc_start = jnp.zeros((tok, tok), jnp.int32)
    end = jnp.int32(0)
    for d in range(docs.shape[0]):
        end = end + docs[d]
        doc_start = jnp.where(query_pos >= end, end, doc_start)
    before = [jnp.int32(0)] * n
    take_q = lax.broadcasted_iota(jnp.int32, (tok, n * slot), 0)
    take_row = lax.broadcasted_iota(jnp.int32, (1, n * slot), 1)
    take = jnp.full((1, n * slot), -1, jnp.int32)
    mine_before = jnp.int32(0)
    for l in range(n):
        start = jnp.int32(0)
        key_pos = jnp.zeros((1, tok), jnp.int32)
        for o in range(n):
            pos = span_pos(jnp.int32(o), lane + (before[o] - start), half, n)
            key_pos = jnp.where(lane >= start, pos, key_pos)
            start = start + counts[l, o]
            before[o] = before[o] + counts[l, o]
        visible = (key_pos <= query_pos) & (key_pos >= doc_start)
        bias[:, l * tok : (l + 1) * tok] = jnp.where(visible, 0.0, -1e30)
        mine = counts[l, me]
        j = take_row - l * slot
        take = jnp.where((j >= 0) & (j < mine), j + mine_before, take)
        mine_before = mine_before + mine
    pick[...] = (take_q == take).astype(jnp.bfloat16)

    for d in range(1, n):
        for direction in (0, 1):

            @pl.when(receives(direction, d) & jnp.logical_not(sends(direction, d)))
            def _():
                wait_kv(direction, d)

    factor = math.log2(math.e) / math.sqrt(HD)
    seq = n * tok
    width = min(seq, 512)
    per = width // tok
    for p in range(parts):
        for d in range(1, n):
            source = lax.rem(me + d, n)
            pltpu.make_async_remote_copy(
                src_ref=qsend.at[p, source],
                dst_ref=qbuf.at[p, source],
                send_sem=q_send_sem.at[0, 0, 0],
                recv_sem=q_recv_sem.at[p, source],
                device_id={"ctx": me},
                device_id_type=MESH,
            ).wait_recv()
        own = jnp.dot(
            pick[...], qbuf[p].reshape(n * slot, PART), preferred_element_type=jnp.float32
        ).astype(jnp.bfloat16)
        for h in range(p * PART // HD, (p + 1) * PART // HD):
            c = h // group
            query = own[:, h * HD - p * PART : (h + 1) * HD - p * PART]
            top = total = acc = None
            for b in range(seq // width):
                key = kbuf[b * per : (b + 1) * per, :, c * HD : (c + 1) * HD].reshape(width, HD)
                value = vbuf[b * per : (b + 1) * per, :, c * HD : (c + 1) * HD].reshape(width, HD)
                score = lax.dot_general(
                    query, key, (((1,), (1,)), ((), ())), preferred_element_type=jnp.float32
                )
                score = score * factor + bias[:, b * width : (b + 1) * width]
                peak = jnp.max(score, axis=1, keepdims=True)
                new = peak if b == 0 else jnp.maximum(top, peak)
                expo = jnp.exp2(score - new)
                part = jnp.sum(expo, axis=1, keepdims=True)
                mixed = jnp.dot(
                    expo.astype(jnp.bfloat16), value, preferred_element_type=jnp.float32
                )
                if b == 0:
                    total, acc = part, mixed
                else:
                    keep = jnp.exp2(top - new)
                    total = total * keep + part
                    acc = acc * keep + mixed
                top = new
            out_ref[:, h * HD : (h + 1) * HD] = (acc / total).astype(jnp.bfloat16)

    for d in range(1, n):
        for direction in (0, 1):

            @pl.when(receives(1 - direction, d))
            def _():
                for p in range(parts):
                    q_copy(direction, d, p).wait_send()

    for d in range(n - 1):
        for direction in (0, 1):

            @pl.when(sends(direction, d))
            def _():
                for copy in kv_copies(direction, d):
                    copy.wait_send()


def body(queries, keys, values, counts, doc_lengths):
    n = lax.axis_size("ctx")
    tok, wide = queries.shape
    narrow = keys.shape[1]
    slot = max(16, 2 * tok // n)
    parts = wide // PART
    vmem = pl.BlockSpec(memory_space=pltpu.VMEM)
    anywhere = pl.BlockSpec(memory_space=pl.ANY)
    return pl.pallas_call(
        functools.partial(kernel, n),
        out_shape=pltpu.VMEM((tok, wide), jnp.bfloat16),
        in_specs=[anywhere] * 5,
        out_specs=vmem,
        scratch_shapes=[
            pltpu.SMEM(counts.shape, jnp.int32),
            pltpu.SMEM(doc_lengths.shape, jnp.int32),
            pltpu.VMEM((tok, wide), jnp.bfloat16),
            pltpu.VMEM((parts, n, slot, PART), jnp.bfloat16),
            pltpu.VMEM((parts, n, slot, PART), jnp.bfloat16),
            pltpu.VMEM((n, tok, narrow), jnp.bfloat16),
            pltpu.VMEM((n, tok, narrow), jnp.bfloat16),
            pltpu.VMEM((tok, n * tok), jnp.float32),
            pltpu.VMEM((tok, n * slot), jnp.bfloat16),
            pltpu.SemaphoreType.DMA((parts, 2, n)),
            pltpu.SemaphoreType.DMA((parts, n)),
            pltpu.SemaphoreType.DMA((2, 2, n)),
            pltpu.SemaphoreType.DMA((2, n)),
            pltpu.SemaphoreType.DMA((5,)),
        ],
        compiler_params=pltpu.CompilerParams(
            collective_id=0, has_side_effects=True, vmem_limit_bytes=56 * 1024 * 1024
        ),
    )(counts, doc_lengths, queries, keys, values)


def solution(mesh):
    placed = (
        P(("dp", "ctx"), "tp"),
        P(("dp", "ctx"), "tp"),
        P(("dp", "ctx"), "tp"),
        P("dp", None),
        P("dp"),
    )
    return jax.shard_map(
        body, mesh=mesh, in_specs=placed, out_specs=P(("dp", "ctx"), "tp"), check_vma=False
    )
```

```python
import functools
import math

import jax
import jax.numpy as jnp
from jax import lax
from jax.experimental import pallas as pl
from jax.experimental.pallas import tpu as pltpu
from jax.sharding import PartitionSpec as P

HQ = 32
KVH = 8
HD = 128
PART = 2 * HD
MESH = pl.DeviceIdType.MESH


def span_pos(owner, local, half, n):
    return jnp.where(
        local < half, owner * half + local, (2 * n - 1 - owner) * half + local - half
    )


def kernel(
    n,
    counts_in,
    docs_in,
    q_in,
    k_in,
    v_in,
    out_ref,
    counts,
    docs,
    q_ref,
    qsend,
    qbuf,
    kbuf,
    vbuf,
    bias,
    pick,
    q_send_sem,
    q_recv_sem,
    kv_send_sem,
    kv_recv_sem,
    load_sem,
):
    me = lax.axis_index("ctx")
    tok = q_ref.shape[0]
    half = tok // 2
    slot = qsend.shape[2]
    parts = q_ref.shape[1] // PART
    group = HQ // KVH

    barrier = pltpu.get_barrier_semaphore()
    for d in range(1, n):
        pl.semaphore_signal(
            barrier, inc=1, device_id={"ctx": lax.rem(me + d, n)}, device_id_type=MESH
        )

    loads = [
        pltpu.make_async_copy(source, target, load_sem.at[i])
        for i, (source, target) in enumerate(
            (
                (k_in, kbuf.at[me]),
                (v_in, vbuf.at[me]),
                (counts_in, counts),
                (docs_in, docs),
                (q_in, q_ref),
            )
        )
    ]
    for load in loads:
        load.start()

    def kv_copies(direction, d):
        sign = 1 if direction == 0 else -1
        source = me - sign * d
        target = me + sign
        return [
            pltpu.make_async_remote_copy(
                src_ref=held.at[source],
                dst_ref=held.at[source],
                send_sem=kv_send_sem.at[which, direction, d],
                recv_sem=kv_recv_sem.at[which, source],
                device_id={"ctx": target},
                device_id_type=MESH,
            )
            for which, held in enumerate((kbuf, vbuf))
        ]

    def sends(direction, d):
        if direction == 0:
            return (me - d >= 0) & (me < n - 1)
        return (me + d < n) & (me > 0)

    def receives(direction, d):
        return (me - d >= 0) if direction == 0 else (me + d < n)

    def wait_kv(direction, d):
        source = me - d if direction == 0 else me + d
        for which, held in enumerate((kbuf, vbuf)):
            pltpu.make_async_remote_copy(
                src_ref=held.at[source],
                dst_ref=held.at[source],
                send_sem=kv_send_sem.at[which, direction, 0],
                recv_sem=kv_recv_sem.at[which, source],
                device_id={"ctx": me},
                device_id_type=MESH,
            ).wait_recv()

    def pass_on(d):
        for direction in (0, 1):

            @pl.when(sends(direction, d))
            def _():
                if d > 0:
                    wait_kv(direction, d)
                for copy in kv_copies(direction, d):
                    copy.start()

    def q_copy(direction, d, p):
        target = me + d if direction == 0 else me - d
        return pltpu.make_async_remote_copy(
            src_ref=qsend.at[p, target],
            dst_ref=qbuf.at[p, me],
            send_sem=q_send_sem.at[p, direction, d],
            recv_sem=q_recv_sem.at[p, me],
            device_id={"ctx": target},
            device_id_type=MESH,
        )

    def at_end(direction, d):
        return (me + d == n - 1) if direction == 0 else (me - d == 0)

    def send_q_ends():
        for p in range(parts):
            for d in range(n - 1, 0, -1):
                for direction in (0, 1):

                    @pl.when(at_end(direction, d))
                    def _():
                        q_copy(direction, d, p).start()

    def send_q_rest():
        for d in range(1, n):
            for direction in (0, 1):

                @pl.when(receives(1 - direction, d) & jnp.logical_not(at_end(direction, d)))
                def _():
                    for p in range(parts):
                        q_copy(direction, d, p).start()

    pl.semaphore_wait(barrier, n - 1)
    loads[0].wait()
    loads[1].wait()
    pass_on(0)
    for load in loads[2:]:
        load.wait()

    row_ids = lax.broadcasted_iota(jnp.int32, (slot, tok), 1)
    row_js = lax.broadcasted_iota(jnp.int32, (slot, tok), 0)
    start = jnp.int32(0)
    onehots = []
    for o in range(n):
        onehots.append((row_ids == row_js + start).astype(jnp.bfloat16))
        start = start + counts[me, o]
    onehot = jnp.concatenate(onehots, axis=0)

    def pack_q(p):
        packed = jnp.dot(
            onehot, q_ref[:, p * PART : (p + 1) * PART], preferred_element_type=jnp.float32
        )
        qsend[p] = packed.astype(jnp.bfloat16).reshape(n, slot, PART)
        qbuf[p, me] = qsend[p, me]

    for p in range(parts):
        pack_q(p)
    send_q_ends()

    local = lax.broadcasted_iota(jnp.int32, (tok, tok), 0)
    lane = lax.broadcasted_iota(jnp.int32, (1, tok), 1)
    query_pos = span_pos(me, local, half, n)
    doc_start = jnp.zeros((tok, tok), jnp.int32)
    end = jnp.int32(0)
    for d in range(docs.shape[0]):
        end = end + docs[d]
        doc_start = jnp.where(query_pos >= end, end, doc_start)
    before = [jnp.int32(0)] * n
    take_q = lax.broadcasted_iota(jnp.int32, (tok, n * slot), 0)
    take_row = lax.broadcasted_iota(jnp.int32, (1, n * slot), 1)
    take = jnp.full((1, n * slot), -1, jnp.int32)
    mine_before = jnp.int32(0)
    for l in range(n):
        start = jnp.int32(0)
        key_pos = jnp.zeros((1, tok), jnp.int32)
        for o in range(n):
            pos = span_pos(jnp.int32(o), lane + (before[o] - start), half, n)
            key_pos = jnp.where(lane >= start, pos, key_pos)
            start = start + counts[l, o]
            before[o] = before[o] + counts[l, o]
        visible = (key_pos <= query_pos) & (key_pos >= doc_start)
        bias[:, l * tok : (l + 1) * tok] = jnp.where(visible, 0.0, -1e30)
        mine = counts[l, me]
        j = take_row - l * slot
        take = jnp.where((j >= 0) & (j < mine), j + mine_before, take)
        mine_before = mine_before + mine
    pick[...] = (take_q == take).astype(jnp.bfloat16)

    for d in range(1, n - 1):
        pass_on(d)
        if d == 1:
            send_q_rest()
    if n < 3:
        send_q_rest()

    for d in range(1, n):
        for direction in (0, 1):

            @pl.when(receives(direction, d) & jnp.logical_not(sends(direction, d)))
            def _():
                wait_kv(direction, d)

    factor = math.log2(math.e) / math.sqrt(HD)
    seq = n * tok
    width = min(seq, 512)
    per = width // tok
    for p in range(parts):
        for d in range(1, n):
            source = lax.rem(me + d, n)
            pltpu.make_async_remote_copy(
                src_ref=qsend.at[p, source],
                dst_ref=qbuf.at[p, source],
                send_sem=q_send_sem.at[0, 0, 0],
                recv_sem=q_recv_sem.at[p, source],
                device_id={"ctx": me},
                device_id_type=MESH,
            ).wait_recv()
        own = jnp.dot(
            pick[...], qbuf[p].reshape(n * slot, PART), preferred_element_type=jnp.float32
        ).astype(jnp.bfloat16)
        for h in range(p * PART // HD, (p + 1) * PART // HD):
            c = h // group
            query = own[:, h * HD - p * PART : (h + 1) * HD - p * PART]
            top = total = acc = None
            for b in range(seq // width):
                key = kbuf[b * per : (b + 1) * per, :, c * HD : (c + 1) * HD].reshape(width, HD)
                value = vbuf[b * per : (b + 1) * per, :, c * HD : (c + 1) * HD].reshape(width, HD)
                score = lax.dot_general(
                    query, key, (((1,), (1,)), ((), ())), preferred_element_type=jnp.float32
                )
                score = score * factor + bias[:, b * width : (b + 1) * width]
                peak = jnp.max(score, axis=1, keepdims=True)
                new = peak if b == 0 else jnp.maximum(top, peak)
                expo = jnp.exp2(score - new)
                part = jnp.sum(expo, axis=1, keepdims=True)
                mixed = jnp.dot(
                    expo.astype(jnp.bfloat16), value, preferred_element_type=jnp.float32
                )
                if b == 0:
                    total, acc = part, mixed
                else:
                    keep = jnp.exp2(top - new)
                    total = total * keep + part
                    acc = acc * keep + mixed
                top = new
            out_ref[:, h * HD : (h + 1) * HD] = (acc / total).astype(jnp.bfloat16)

    for d in range(1, n):
        for direction in (0, 1):

            @pl.when(receives(1 - direction, d))
            def _():
                for p in range(parts):
                    q_copy(direction, d, p).wait_send()

    for d in range(n - 1):
        for direction in (0, 1):

            @pl.when(sends(direction, d))
            def _():
                for copy in kv_copies(direction, d):
                    copy.wait_send()


def body(queries, keys, values, counts, doc_lengths):
    n = lax.axis_size("ctx")
    tok, wide = queries.shape
    narrow = keys.shape[1]
    slot = max(16, 2 * tok // n)
    parts = wide // PART
    vmem = pl.BlockSpec(memory_space=pltpu.VMEM)
    anywhere = pl.BlockSpec(memory_space=pl.ANY)
    return pl.pallas_call(
        functools.partial(kernel, n),
        out_shape=pltpu.VMEM((tok, wide), jnp.bfloat16),
        in_specs=[anywhere] * 5,
        out_specs=vmem,
        scratch_shapes=[
            pltpu.SMEM(counts.shape, jnp.int32),
            pltpu.SMEM(doc_lengths.shape, jnp.int32),
            pltpu.VMEM((tok, wide), jnp.bfloat16),
            pltpu.VMEM((parts, n, slot, PART), jnp.bfloat16),
            pltpu.VMEM((parts, n, slot, PART), jnp.bfloat16),
            pltpu.VMEM((n, tok, narrow), jnp.bfloat16),
            pltpu.VMEM((n, tok, narrow), jnp.bfloat16),
            pltpu.VMEM((tok, n * tok), jnp.float32),
            pltpu.VMEM((tok, n * slot), jnp.bfloat16),
            pltpu.SemaphoreType.DMA((parts, 2, n)),
            pltpu.SemaphoreType.DMA((parts, n)),
            pltpu.SemaphoreType.DMA((2, 2, n)),
            pltpu.SemaphoreType.DMA((2, n)),
            pltpu.SemaphoreType.DMA((5,)),
        ],
        compiler_params=pltpu.CompilerParams(
            collective_id=0, has_side_effects=True, vmem_limit_bytes=56 * 1024 * 1024
        ),
    )(counts, doc_lengths, queries, keys, values)


def solution(mesh):
    placed = (
        P(("dp", "ctx"), "tp"),
        P(("dp", "ctx"), "tp"),
        P(("dp", "ctx"), "tp"),
        P("dp", None),
        P("dp"),
    )
    return jax.shard_map(
        body, mesh=mesh, in_specs=placed, out_specs=P(("dp", "ctx"), "tp"), check_vma=False
    )
```

```python
import functools
import math

import jax
import jax.numpy as jnp
from jax import lax
from jax.experimental import pallas as pl
from jax.experimental.pallas import tpu as pltpu
from jax.sharding import PartitionSpec as P

HQ = 32
KVH = 8
HD = 128
PART = 2 * HD
MESH = pl.DeviceIdType.MESH


def span_pos(owner, local, half, n):
    return jnp.where(
        local < half, owner * half + local, (2 * n - 1 - owner) * half + local - half
    )


def kernel(
    n,
    counts_in,
    docs_in,
    q_in,
    k_in,
    v_in,
    out_ref,
    counts,
    docs,
    q_ref,
    qsend,
    qbuf,
    kbuf,
    vbuf,
    bias,
    pick,
    rbuf,
    rpick,
    merged,
    obuf,
    own,
    q_send_sem,
    q_recv_sem,
    kv_send_sem,
    kv_recv_sem,
    load_sem,
    r_recv_sem,
    o_send_sem,
    o_recv_sem,
):
    me = lax.axis_index("ctx")
    tok = q_ref.shape[0]
    half = tok // 2
    slot = qsend.shape[2]
    parts = q_ref.shape[1] // PART
    group = HQ // KVH
    is_end = (me == 0) | (me == n - 1)
    is_relay = (me == 1) | (me == n - 2)
    end_id = jnp.where(me == 1, 0, n - 1)

    barrier = pltpu.get_barrier_semaphore()
    for d in range(1, n):
        pl.semaphore_signal(
            barrier, inc=1, device_id={"ctx": lax.rem(me + d, n)}, device_id_type=MESH
        )

    loads = [
        pltpu.make_async_copy(source, target, load_sem.at[i])
        for i, (source, target) in enumerate(
            (
                (k_in, kbuf.at[me]),
                (v_in, vbuf.at[me]),
                (counts_in, counts),
                (docs_in, docs),
                (q_in, q_ref),
            )
        )
    ]
    for load in loads:
        load.start()

    def kv_copies(direction, d):
        sign = 1 if direction == 0 else -1
        source = me - sign * d
        target = me + sign
        return [
            pltpu.make_async_remote_copy(
                src_ref=held.at[source],
                dst_ref=held.at[source],
                send_sem=kv_send_sem.at[which, direction, d],
                recv_sem=kv_recv_sem.at[which, source],
                device_id={"ctx": target},
                device_id_type=MESH,
            )
            for which, held in enumerate((kbuf, vbuf))
        ]

    def sends(direction, d):
        if direction == 0:
            return (me - d >= 0) & (me < n - 1)
        return (me + d < n) & (me > 0)

    def receives(direction, d):
        return (me - d >= 0) if direction == 0 else (me + d < n)

    def wait_kv(direction, d):
        source = me - d if direction == 0 else me + d
        for which, held in enumerate((kbuf, vbuf)):
            pltpu.make_async_remote_copy(
                src_ref=held.at[source],
                dst_ref=held.at[source],
                send_sem=kv_send_sem.at[which, direction, 0],
                recv_sem=kv_recv_sem.at[which, source],
                device_id={"ctx": me},
                device_id_type=MESH,
            ).wait_recv()

    def pass_on(d):
        for direction in (0, 1):

            @pl.when(sends(direction, d))
            def _():
                if d > 0:
                    wait_kv(direction, d)
                for copy in kv_copies(direction, d):
                    copy.start()

    def q_copy(direction, d, p):
        target = me + d if direction == 0 else me - d
        return pltpu.make_async_remote_copy(
            src_ref=qsend.at[p, target],
            dst_ref=qbuf.at[p, me],
            send_sem=q_send_sem.at[p, direction, d],
            recv_sem=q_recv_sem.at[p, me],
            device_id={"ctx": target},
            device_id_type=MESH,
        )

    def at_end(direction, d):
        return (me + d == n - 1) if direction == 0 else (me - d == 0)

    def end_copy(direction, d, p):
        return pltpu.make_async_remote_copy(
            src_ref=qsend.at[p, n - 1 if direction == 0 else 0],
            dst_ref=rbuf.at[p, me],
            send_sem=q_send_sem.at[p, direction, d],
            recv_sem=r_recv_sem.at[p, me],
            device_id={"ctx": n - 2 if direction == 0 else 1},
            device_id_type=MESH,
        )

    def merged_copy(p):
        return pltpu.make_async_remote_copy(
            src_ref=merged.at[p],
            dst_ref=obuf.at[p],
            send_sem=o_send_sem.at[p],
            recv_sem=o_recv_sem.at[p],
            device_id={"ctx": end_id},
            device_id_type=MESH,
        )

    def merge(p):
        for d in range(1, n):
            source = lax.rem(me + d, n)

            @pl.when(source != end_id)
            def _():
                pltpu.make_async_remote_copy(
                    src_ref=rbuf.at[p, source],
                    dst_ref=rbuf.at[p, source],
                    send_sem=q_send_sem.at[0, 0, 0],
                    recv_sem=r_recv_sem.at[p, source],
                    device_id={"ctx": me},
                    device_id_type=MESH,
                ).wait_recv()

        merged[p] = jnp.dot(
            rpick[...], rbuf[p].reshape(n * slot, PART), preferred_element_type=jnp.float32
        ).astype(jnp.bfloat16)
        merged_copy(p).start()

    def send_q_ends():
        for p in range(parts):
            for d in range(n - 1, 1, -1):
                for direction in (0, 1):

                    @pl.when(at_end(direction, d))
                    def _():
                        end_copy(direction, d, p).start()

    def send_q_rest():
        for d in range(1, n):
            for direction in (0, 1):

                @pl.when(receives(1 - direction, d) & jnp.logical_not(at_end(direction, d)))
                def _():
                    for p in range(parts):
                        q_copy(direction, d, p).start()

    pl.semaphore_wait(barrier, n - 1)
    loads[0].wait()
    loads[1].wait()
    pass_on(0)
    for load in loads[2:]:
        load.wait()

    row_ids = lax.broadcasted_iota(jnp.int32, (slot, tok), 1)
    row_js = lax.broadcasted_iota(jnp.int32, (slot, tok), 0)
    start = jnp.int32(0)
    onehots = []
    for o in range(n):
        onehots.append((row_ids == row_js + start).astype(jnp.bfloat16))
        start = start + counts[me, o]
    onehot = jnp.concatenate(onehots, axis=0)

    def pack_q(p):
        packed = jnp.dot(
            onehot, q_ref[:, p * PART : (p + 1) * PART], preferred_element_type=jnp.float32
        )
        qsend[p] = packed.astype(jnp.bfloat16).reshape(n, slot, PART)

    for p in range(parts):
        pack_q(p)
    send_q_ends()

    @pl.when(is_end)
    def _():
        qbuf[...] = jnp.zeros_like(qbuf)

    @pl.when(is_relay)
    def _():
        for p in range(parts):
            rbuf[p, me] = qsend[p, end_id]
            rbuf[p, end_id] = jnp.zeros((slot, PART), jnp.bfloat16)

    for p in range(parts):
        qbuf[p, me] = qsend[p, me]

    local = lax.broadcasted_iota(jnp.int32, (tok, tok), 0)
    lane = lax.broadcasted_iota(jnp.int32, (1, tok), 1)
    query_pos = span_pos(me, local, half, n)
    doc_start = jnp.zeros((tok, tok), jnp.int32)
    end = jnp.int32(0)
    for d in range(docs.shape[0]):
        end = end + docs[d]
        doc_start = jnp.where(query_pos >= end, end, doc_start)
    before = [jnp.int32(0)] * n
    take_q = lax.broadcasted_iota(jnp.int32, (tok, n * slot), 0)
    take_row = lax.broadcasted_iota(jnp.int32, (1, n * slot), 1)
    take = jnp.full((1, n * slot), -1, jnp.int32)
    mine_before = jnp.int32(0)
    end_take = take
    end_before = jnp.int32(0)
    for l in range(n):
        start = jnp.int32(0)
        key_pos = jnp.zeros((1, tok), jnp.int32)
        for o in range(n):
            pos = span_pos(jnp.int32(o), lane + (before[o] - start), half, n)
            key_pos = jnp.where(lane >= start, pos, key_pos)
            start = start + counts[l, o]
            before[o] = before[o] + counts[l, o]
        visible = (key_pos <= query_pos) & (key_pos >= doc_start)
        bias[:, l * tok : (l + 1) * tok] = jnp.where(visible, 0.0, -1e30)
        mine = counts[l, me]
        j = take_row - l * slot
        take = jnp.where((j >= 0) & (j < mine), j + mine_before, take)
        mine_before = mine_before + mine
        theirs = counts[l, end_id]
        end_take = jnp.where((j >= 0) & (j < theirs), j + end_before, end_take)
        end_before = end_before + theirs
    pick[...] = (take_q == take).astype(jnp.bfloat16)
    rpick[...] = (take_q == end_take).astype(jnp.bfloat16)

    for d in range(1, n - 1):
        pass_on(d)
        if d == 1:
            send_q_rest()

    @pl.when(is_relay)
    def _():
        for p in range(parts):
            merge(p)

    for d in range(1, n):
        for direction in (0, 1):

            @pl.when(receives(direction, d) & jnp.logical_not(sends(direction, d)))
            def _():
                wait_kv(direction, d)

    factor = math.log2(math.e) / math.sqrt(HD)
    seq = n * tok
    width = min(seq, 512)
    per = width // tok
    for p in range(parts):
        @pl.when(jnp.logical_not(is_end))
        def _():
            for d in range(1, n):
                source = lax.rem(me + d, n)
                pltpu.make_async_remote_copy(
                    src_ref=qsend.at[p, source],
                    dst_ref=qbuf.at[p, source],
                    send_sem=q_send_sem.at[0, 0, 0],
                    recv_sem=q_recv_sem.at[p, source],
                    device_id={"ctx": me},
                    device_id_type=MESH,
                ).wait_recv()

        own[...] = jnp.dot(
            pick[...], qbuf[p].reshape(n * slot, PART), preferred_element_type=jnp.float32
        ).astype(jnp.bfloat16)

        @pl.when(is_end)
        def _():
            merged_copy(p).wait_recv()
            own[...] = own[...] + obuf[p]

        for h in range(p * PART // HD, (p + 1) * PART // HD):
            c = h // group
            query = own[:, h * HD - p * PART : (h + 1) * HD - p * PART]
            top = total = acc = None
            for b in range(seq // width):
                key = kbuf[b * per : (b + 1) * per, :, c * HD : (c + 1) * HD].reshape(width, HD)
                value = vbuf[b * per : (b + 1) * per, :, c * HD : (c + 1) * HD].reshape(width, HD)
                score = lax.dot_general(
                    query, key, (((1,), (1,)), ((), ())), preferred_element_type=jnp.float32
                )
                score = score * factor + bias[:, b * width : (b + 1) * width]
                peak = jnp.max(score, axis=1, keepdims=True)
                new = peak if b == 0 else jnp.maximum(top, peak)
                expo = jnp.exp2(score - new)
                part = jnp.sum(expo, axis=1, keepdims=True)
                mixed = jnp.dot(
                    expo.astype(jnp.bfloat16), value, preferred_element_type=jnp.float32
                )
                if b == 0:
                    total, acc = part, mixed
                else:
                    keep = jnp.exp2(top - new)
                    total = total * keep + part
                    acc = acc * keep + mixed
                top = new
            out_ref[:, h * HD : (h + 1) * HD] = (acc / total).astype(jnp.bfloat16)

    for d in range(1, n):
        for direction in (0, 1):

            @pl.when(receives(1 - direction, d) & jnp.logical_not(at_end(direction, d)))
            def _():
                for p in range(parts):
                    q_copy(direction, d, p).wait_send()

            if d > 1:

                @pl.when(at_end(direction, d))
                def _():
                    for p in range(parts):
                        end_copy(direction, d, p).wait_send()

    @pl.when(is_relay)
    def _():
        for p in range(parts):
            merged_copy(p).wait_send()

    for d in range(n - 1):
        for direction in (0, 1):

            @pl.when(sends(direction, d))
            def _():
                for copy in kv_copies(direction, d):
                    copy.wait_send()


def body(queries, keys, values, counts, doc_lengths):
    n = lax.axis_size("ctx")
    tok, wide = queries.shape
    narrow = keys.shape[1]
    slot = max(16, 2 * tok // n)
    parts = wide // PART
    vmem = pl.BlockSpec(memory_space=pltpu.VMEM)
    anywhere = pl.BlockSpec(memory_space=pl.ANY)
    return pl.pallas_call(
        functools.partial(kernel, n),
        out_shape=pltpu.VMEM((tok, wide), jnp.bfloat16),
        in_specs=[anywhere] * 5,
        out_specs=vmem,
        scratch_shapes=[
            pltpu.SMEM(counts.shape, jnp.int32),
            pltpu.SMEM(doc_lengths.shape, jnp.int32),
            pltpu.VMEM((tok, wide), jnp.bfloat16),
            pltpu.VMEM((parts, n, slot, PART), jnp.bfloat16),
            pltpu.VMEM((parts, n, slot, PART), jnp.bfloat16),
            pltpu.VMEM((n, tok, narrow), jnp.bfloat16),
            pltpu.VMEM((n, tok, narrow), jnp.bfloat16),
            pltpu.VMEM((tok, n * tok), jnp.float32),
            pltpu.VMEM((tok, n * slot), jnp.bfloat16),
            pltpu.VMEM((parts, n, slot, PART), jnp.bfloat16),
            pltpu.VMEM((tok, n * slot), jnp.bfloat16),
            pltpu.VMEM((parts, tok, PART), jnp.bfloat16),
            pltpu.VMEM((parts, tok, PART), jnp.bfloat16),
            pltpu.VMEM((tok, PART), jnp.bfloat16),
            pltpu.SemaphoreType.DMA((parts, 2, n)),
            pltpu.SemaphoreType.DMA((parts, n)),
            pltpu.SemaphoreType.DMA((2, 2, n)),
            pltpu.SemaphoreType.DMA((2, n)),
            pltpu.SemaphoreType.DMA((5,)),
            pltpu.SemaphoreType.DMA((parts, n)),
            pltpu.SemaphoreType.DMA((parts,)),
            pltpu.SemaphoreType.DMA((parts,)),
        ],
        compiler_params=pltpu.CompilerParams(
            collective_id=0, has_side_effects=True, vmem_limit_bytes=56 * 1024 * 1024
        ),
    )(counts, doc_lengths, queries, keys, values)


def solution(mesh):
    placed = (
        P(("dp", "ctx"), "tp"),
        P(("dp", "ctx"), "tp"),
        P(("dp", "ctx"), "tp"),
        P("dp", None),
        P("dp"),
    )
    return jax.shard_map(
        body, mesh=mesh, in_specs=placed, out_specs=P(("dp", "ctx"), "tp"), check_vma=False
    )
```

```python
import functools
import math

import jax
import jax.numpy as jnp
from jax import lax
from jax.experimental import pallas as pl
from jax.experimental.pallas import tpu as pltpu
from jax.sharding import PartitionSpec as P

HQ = 32
KVH = 8
HD = 128
PART = 4 * HD
MESH = pl.DeviceIdType.MESH


def span_pos(owner, local, half, n):
    return jnp.where(
        local < half, owner * half + local, (2 * n - 1 - owner) * half + local - half
    )


def kernel(
    n,
    counts_in,
    docs_in,
    q_in,
    k_in,
    v_in,
    out_ref,
    counts,
    docs,
    q_ref,
    qsend,
    qbuf,
    kbuf,
    vbuf,
    bias,
    pick,
    q_send_sem,
    q_recv_sem,
    kv_send_sem,
    kv_recv_sem,
    load_sem,
):
    me = lax.axis_index("ctx")
    tok = q_ref.shape[0]
    half = tok // 2
    slot = qsend.shape[2]
    parts = q_ref.shape[1] // PART
    group = HQ // KVH

    barrier = pltpu.get_barrier_semaphore()
    for d in range(1, n):
        pl.semaphore_signal(
            barrier, inc=1, device_id={"ctx": lax.rem(me + d, n)}, device_id_type=MESH
        )

    loads = [
        pltpu.make_async_copy(source, target, load_sem.at[i])
        for i, (source, target) in enumerate(
            (
                (k_in, kbuf.at[me]),
                (v_in, vbuf.at[me]),
                (counts_in, counts),
                (docs_in, docs),
                (q_in, q_ref),
            )
        )
    ]
    for load in loads:
        load.start()

    def kv_copies(direction, d):
        sign = 1 if direction == 0 else -1
        source = me - sign * d
        target = me + sign
        return [
            pltpu.make_async_remote_copy(
                src_ref=held.at[source],
                dst_ref=held.at[source],
                send_sem=kv_send_sem.at[which, direction, d],
                recv_sem=kv_recv_sem.at[which, source],
                device_id={"ctx": target},
                device_id_type=MESH,
            )
            for which, held in enumerate((kbuf, vbuf))
        ]

    def sends(direction, d):
        if direction == 0:
            return (me - d >= 0) & (me < n - 1)
        return (me + d < n) & (me > 0)

    def receives(direction, d):
        return (me - d >= 0) if direction == 0 else (me + d < n)

    def wait_kv(direction, d):
        source = me - d if direction == 0 else me + d
        for which, held in enumerate((kbuf, vbuf)):
            pltpu.make_async_remote_copy(
                src_ref=held.at[source],
                dst_ref=held.at[source],
                send_sem=kv_send_sem.at[which, direction, 0],
                recv_sem=kv_recv_sem.at[which, source],
                device_id={"ctx": me},
                device_id_type=MESH,
            ).wait_recv()

    def pass_on(d):
        for direction in (0, 1):

            @pl.when(sends(direction, d))
            def _():
                if d > 0:
                    wait_kv(direction, d)
                for copy in kv_copies(direction, d):
                    copy.start()

    def q_copy(direction, d, p):
        target = me + d if direction == 0 else me - d
        return pltpu.make_async_remote_copy(
            src_ref=qsend.at[p, target],
            dst_ref=qbuf.at[p, me],
            send_sem=q_send_sem.at[p, direction, d],
            recv_sem=q_recv_sem.at[p, me],
            device_id={"ctx": target},
            device_id_type=MESH,
        )

    def send_q(d):
        for direction in (0, 1):

            @pl.when(receives(1 - direction, d))
            def _():
                for p in range(parts):
                    q_copy(direction, d, p).start()

    pl.semaphore_wait(barrier, n - 1)
    loads[0].wait()
    loads[1].wait()
    pass_on(0)
    for load in loads[2:]:
        load.wait()

    row_ids = lax.broadcasted_iota(jnp.int32, (slot, tok), 1)
    row_js = lax.broadcasted_iota(jnp.int32, (slot, tok), 0)
    start = jnp.int32(0)
    onehots = []
    for o in range(n):
        onehots.append((row_ids == row_js + start).astype(jnp.bfloat16))
        start = start + counts[me, o]
    onehot = jnp.concatenate(onehots, axis=0)

    def pack_q(p):
        packed = jnp.dot(
            onehot, q_ref[:, p * PART : (p + 1) * PART], preferred_element_type=jnp.float32
        )
        qsend[p] = packed.astype(jnp.bfloat16).reshape(n, slot, PART)
        qbuf[p, me] = qsend[p, me]

    for p in range(parts):
        pack_q(p)
    for d in range(n - 1, 1, -1):
        send_q(d)
    for d in range(1, n - 1):
        pass_on(d)
        if d == 1:
            send_q(1)

    local = lax.broadcasted_iota(jnp.int32, (tok, tok), 0)
    lane = lax.broadcasted_iota(jnp.int32, (1, tok), 1)
    query_pos = span_pos(me, local, half, n)
    doc_start = jnp.zeros((tok, tok), jnp.int32)
    end = jnp.int32(0)
    for d in range(docs.shape[0]):
        end = end + docs[d]
        doc_start = jnp.where(query_pos >= end, end, doc_start)
    before = [jnp.int32(0)] * n
    take_q = lax.broadcasted_iota(jnp.int32, (tok, n * slot), 0)
    take_row = lax.broadcasted_iota(jnp.int32, (1, n * slot), 1)
    take = jnp.full((1, n * slot), -1, jnp.int32)
    mine_before = jnp.int32(0)
    for l in range(n):
        start = jnp.int32(0)
        key_pos = jnp.zeros((1, tok), jnp.int32)
        for o in range(n):
            pos = span_pos(jnp.int32(o), lane + (before[o] - start), half, n)
            key_pos = jnp.where(lane >= start, pos, key_pos)
            start = start + counts[l, o]
            before[o] = before[o] + counts[l, o]
        visible = (key_pos <= query_pos) & (key_pos >= doc_start)
        bias[:, l * tok : (l + 1) * tok] = jnp.where(visible, 0.0, -1e30)
        mine = counts[l, me]
        j = take_row - l * slot
        take = jnp.where((j >= 0) & (j < mine), j + mine_before, take)
        mine_before = mine_before + mine
    pick[...] = (take_q == take).astype(jnp.bfloat16)

    for d in range(1, n):
        for direction in (0, 1):

            @pl.when(receives(direction, d) & jnp.logical_not(sends(direction, d)))
            def _():
                wait_kv(direction, d)

    factor = math.log2(math.e) / math.sqrt(HD)
    seq = n * tok
    width = min(seq, 512)
    per = width // tok
    for p in range(parts):
        for d in range(1, n):
            source = lax.rem(me + d, n)
            pltpu.make_async_remote_copy(
                src_ref=qsend.at[p, source],
                dst_ref=qbuf.at[p, source],
                send_sem=q_send_sem.at[0, 0, 0],
                recv_sem=q_recv_sem.at[p, source],
                device_id={"ctx": me},
                device_id_type=MESH,
            ).wait_recv()
        own = jnp.dot(
            pick[...], qbuf[p].reshape(n * slot, PART), preferred_element_type=jnp.float32
        ).astype(jnp.bfloat16)
        for h in range(p * PART // HD, (p + 1) * PART // HD):
            c = h // group
            query = own[:, h * HD - p * PART : (h + 1) * HD - p * PART]
            top = total = acc = None
            for b in range(seq // width):
                key = kbuf[b * per : (b + 1) * per, :, c * HD : (c + 1) * HD].reshape(width, HD)
                value = vbuf[b * per : (b + 1) * per, :, c * HD : (c + 1) * HD].reshape(width, HD)
                score = lax.dot_general(
                    query, key, (((1,), (1,)), ((), ())), preferred_element_type=jnp.float32
                )
                score = score * factor + bias[:, b * width : (b + 1) * width]
                peak = jnp.max(score, axis=1, keepdims=True)
                new = peak if b == 0 else jnp.maximum(top, peak)
                expo = jnp.exp2(score - new)
                part = jnp.sum(expo, axis=1, keepdims=True)
                mixed = jnp.dot(
                    expo.astype(jnp.bfloat16), value, preferred_element_type=jnp.float32
                )
                if b == 0:
                    total, acc = part, mixed
                else:
                    keep = jnp.exp2(top - new)
                    total = total * keep + part
                    acc = acc * keep + mixed
                top = new
            out_ref[:, h * HD : (h + 1) * HD] = (acc / total).astype(jnp.bfloat16)

    for d in range(1, n):
        for direction in (0, 1):

            @pl.when(receives(1 - direction, d))
            def _():
                for p in range(parts):
                    q_copy(direction, d, p).wait_send()

    for d in range(n - 1):
        for direction in (0, 1):

            @pl.when(sends(direction, d))
            def _():
                for copy in kv_copies(direction, d):
                    copy.wait_send()


def body(queries, keys, values, counts, doc_lengths):
    n = lax.axis_size("ctx")
    tok, wide = queries.shape
    narrow = keys.shape[1]
    slot = max(16, 2 * tok // n)
    parts = wide // PART
    vmem = pl.BlockSpec(memory_space=pltpu.VMEM)
    anywhere = pl.BlockSpec(memory_space=pl.ANY)
    return pl.pallas_call(
        functools.partial(kernel, n),
        out_shape=pltpu.VMEM((tok, wide), jnp.bfloat16),
        in_specs=[anywhere] * 5,
        out_specs=vmem,
        scratch_shapes=[
            pltpu.SMEM(counts.shape, jnp.int32),
            pltpu.SMEM(doc_lengths.shape, jnp.int32),
            pltpu.VMEM((tok, wide), jnp.bfloat16),
            pltpu.VMEM((parts, n, slot, PART), jnp.bfloat16),
            pltpu.VMEM((parts, n, slot, PART), jnp.bfloat16),
            pltpu.VMEM((n, tok, narrow), jnp.bfloat16),
            pltpu.VMEM((n, tok, narrow), jnp.bfloat16),
            pltpu.VMEM((tok, n * tok), jnp.float32),
            pltpu.VMEM((tok, n * slot), jnp.bfloat16),
            pltpu.SemaphoreType.DMA((parts, 2, n)),
            pltpu.SemaphoreType.DMA((parts, n)),
            pltpu.SemaphoreType.DMA((2, 2, n)),
            pltpu.SemaphoreType.DMA((2, n)),
            pltpu.SemaphoreType.DMA((5,)),
        ],
        compiler_params=pltpu.CompilerParams(
            collective_id=0, has_side_effects=True, vmem_limit_bytes=56 * 1024 * 1024
        ),
    )(counts, doc_lengths, queries, keys, values)


def solution(mesh):
    placed = (
        P(("dp", "ctx"), "tp"),
        P(("dp", "ctx"), "tp"),
        P(("dp", "ctx"), "tp"),
        P("dp", None),
        P("dp"),
    )
    return jax.shard_map(
        body, mesh=mesh, in_specs=placed, out_specs=P(("dp", "ctx"), "tp"), check_vma=False
    )
```
